32 devices in a mesh: pix: 8 (over z, x), tm: 4 (over y, core).
Axes of the slice: x: 2, y: 2, z: 4, core: 2. Of those that a mesh axis runs over, the one named last changes fastest.
Arguments:
- query: bfloat16 [4, 8, 1024, 1152], P('tm', 'pix'), may hold values from -5 to 5, as said below
- key_in: bfloat16 [4, 8, 1024, 1152], P('tm', 'pix'), may hold values from -5 to 5, as said below
- value: bfloat16 [4, 8, 1024, 1152], P('tm', 'pix'), may hold values from -6 to 6
- mask: int32 [8, 8], replicated, may hold values from 0 to 1, as said below
- w_out: bfloat16 [1152, 1152], replicated, may hold values from -0.1875 to 0.1875
Outputs:
- result: bfloat16 [4, 8, 1024, 1152], P('tm', 'pix')
The draws below stay inside these ranges and needn't reach their ends.
Inputs may be any that keep to these rules, and one draw needn't show every extreme that they name: `mask`: the diagonal is 1 everywhere; the table is a dilated pattern of block pairs with some further pairs set. `query`: entries of order one. `key_in`: entries of order one.
All inputs are finite; a program needn't handle non-finite values.
Results may differ from the reference program's by a relative error of at most 0.012.
Values may be sent and summed in bfloat16 or wider, within the bound.
No kernel may reach another device: no remote copies, remote signals or barrier semaphores. Data moves between devices by JAX's collectives and lax.ppermute only.
A program may use at most 192 MiB of HBM per device.

```python
import jax
import jax.numpy as jnp
from jax import lax

C = 1152
HEADS = 16
HDIM = 72
NBLK = 8
PIXELS = 1024
FTM = 8
FRAMES = 32
N_TM = 4


def draw_query(key, part):
    key = jax.random.fold_in(key, 1)
    drawn = jnp.clip(jax.random.normal(key, (FRAMES, PIXELS, C), jnp.float32), -5.0, 5.0)
    return drawn.reshape(N_TM, FTM, PIXELS, C).astype(jnp.bfloat16)


def draw_key_in(key, part):
    key = jax.random.fold_in(key, 2)
    drawn = jnp.clip(jax.random.normal(key, (FRAMES, PIXELS, C), jnp.float32), -5.0, 5.0)
    return drawn.reshape(N_TM, FTM, PIXELS, C).astype(jnp.bfloat16)


def draw_mask(key, part):
    key = jax.random.fold_in(key, 7)
    first_key, second_key = jax.random.split(key)
    dilation = jax.random.randint(first_key, (), 2, 4)
    index = jnp.arange(NBLK, dtype=jnp.int32)
    apart = (index[:, None] - index[None, :]) % dilation
    extra = jax.random.randint(second_key, (NBLK, NBLK), 0, 4) == 0
    return jnp.where((apart == 0) | extra, 1, 0).astype(jnp.int32)


def steps_of(own_key, extent, shards, least, high):
    def one(position, blocks):
        steps = jax.random.uniform(jax.random.fold_in(jax.random.fold_in(own_key, 6), position), (blocks,), jnp.float32, least / len(shards), high / len(shards))
        return jnp.repeat(jnp.exp(steps), extent[position] // blocks).reshape((-1,) + (1,) * (len(extent) - position - 1))

    gain = one(*shards[0])
    for cut in shards[1:]:
        gain = gain * one(*cut)
    return gain


def bell_draw(rng, shape, width, bound, cuts=(), kind=jnp.bfloat16):
    values = jax.random.normal(rng, shape, jnp.float32) * width
    if len(cuts) > 0:
        values = steps_of(rng, shape, cuts, -0.22, 0.18) * values
    return jnp.clip(values, min=-bound, max=bound).astype(kind)


def setup_inputs(seed: int = 0) -> dict:
    streams_of = jax.random.split(jax.random.key(seed), 6)
    return {
        "query": draw_query(jax.random.fold_in(streams_of[5], 71), 0),
        "key_in": draw_key_in(jax.random.fold_in(streams_of[5], 71), 0),
        "value": bell_draw(streams_of[2], (N_TM, FTM, PIXELS, C), 1.0, 6.0, ((0, 4), (1, 8))),
        "mask": draw_mask(jax.random.fold_in(streams_of[5], 71), 0),
        "w_out": bell_draw(streams_of[4], (C, C), C ** -0.5, 0.1875),
    }


def reference(query, key_in, value, mask, w_out):
    group = 16
    scale = 1.0 / (HDIM ** 0.5)
    blen = FRAMES // NBLK
    block_of = jnp.arange(FRAMES, dtype=jnp.int32) // blen
    allowed = mask[block_of][:, block_of] > 0

    def split_groups(arr):
        shaped = arr.reshape(FRAMES, PIXELS // group, group, HEADS, HDIM)
        return jnp.moveaxis(shaped, 1, 0)

    def one_group(items):
        qg, kg, vg = items
        scores = jnp.einsum("iphd,jphd->phij", qg.astype(jnp.float32), kg.astype(jnp.float32)) * scale
        masked = jnp.where(allowed, scores, -1e30)
        top = jnp.max(masked, axis=-1, keepdims=True)
        expo = jnp.where(allowed, jnp.exp(scores - top), 0.0)
        total = jnp.sum(expo, axis=-1)
        weights = expo.astype(jnp.bfloat16)
        summed = jnp.einsum("phij,jphd->iphd", weights.astype(jnp.float32), vg.astype(jnp.float32))
        return (summed / jnp.transpose(total, (2, 0, 1))[..., None]).astype(jnp.bfloat16)

    attended = lax.map(one_group, (split_groups(query), split_groups(key_in), split_groups(value)))
    attended = jnp.moveaxis(attended, 0, 1).reshape(FRAMES * PIXELS, C)
    result = jnp.dot(attended, w_out, preferred_element_type=jnp.float32).astype(jnp.bfloat16)
    return result.reshape(N_TM, FTM, PIXELS, C)
```

```python
import functools
import math

import jax
import jax.numpy as jnp
from jax import lax
from jax.experimental import pallas as pl
from jax.experimental.pallas import tpu as pltpu
from jax.sharding import PartitionSpec as P

HDIM = 72
LANES = 128
SUB = 8


def attend_kernel(qkv_ref, bias_ref, w_ref, out_ref, acc_ref):
    frames, _, _, sub, feats = qkv_ref.shape
    rows = frames * sub
    scale = math.log2(math.e) / HDIM**0.5
    for head in range(feats // HDIM):
        low, high = head * HDIM, (head + 1) * HDIM
        start, stop = low // LANES * LANES, -(-high // LANES) * LANES
        lane = lax.broadcasted_iota(jnp.int32, (1, stop - start), 1) + start
        mine = (lane >= low) & (lane < high)
        q = qkv_ref[:, 0, 0, :, start:stop].reshape(rows, stop - start)
        k = qkv_ref[:, 0, 1, :, start:stop].reshape(rows, stop - start)
        v = qkv_ref[:, 0, 2, :, start:stop].reshape(rows, stop - start)
        q = jnp.where(mine, q, jnp.zeros_like(q))
        scores = lax.dot_general(q, k, (((1,), (1,)), ((), ())), preferred_element_type=jnp.float32)
        scores = scores * scale + bias_ref[...]
        expo = jnp.exp2(scores - jnp.max(scores, axis=1, keepdims=True))
        total = jnp.sum(expo, axis=1, keepdims=True)
        summed = jnp.dot(expo.astype(jnp.bfloat16), v, preferred_element_type=jnp.float32)
        acc_ref[:, start:stop] = jnp.where(mine, summed / total, acc_ref[:, start:stop])
    attended = acc_ref[...].astype(jnp.bfloat16)
    projected = jnp.dot(attended, w_ref[...], preferred_element_type=jnp.float32)
    out_ref[...] = projected.astype(jnp.bfloat16).reshape(out_ref.shape)


def attend(qkv, bias, w_out):
    frames, groups, _, sub, feats = qkv.shape
    rows = frames * sub
    return pl.pallas_call(
        attend_kernel,
        grid=(groups,),
        in_specs=[
            pl.BlockSpec((frames, 1, 3, sub, feats), lambda g: (0, g, 0, 0, 0)),
            pl.BlockSpec((rows, rows), lambda g: (0, 0)),
            pl.BlockSpec((feats, feats), lambda g: (0, 0)),
        ],
        out_specs=pl.BlockSpec((frames, 1, sub, feats), lambda g: (0, g, 0, 0)),
        out_shape=jax.ShapeDtypeStruct((frames, groups, sub, feats), jnp.bfloat16),
        scratch_shapes=[pltpu.VMEM((rows, feats), jnp.float32)],
        compiler_params=pltpu.CompilerParams(vmem_limit_bytes=48 * 2**20),
        cost_estimate=pl.CostEstimate(
            flops=groups * rows * feats * (feats + 4 * rows) * 2, bytes_accessed=groups * rows * feats * 8, transcendentals=0
        ),
    )(qkv, bias, w_out)


def bias_of(mask, frame_of_row, patch_of_row, blen):
    block = frame_of_row // blen
    allowed = (mask[block][:, block] > 0) & (patch_of_row[:, None] == patch_of_row[None, :])
    return jnp.where(allowed, 0.0, -1e30).astype(jnp.float32)


def plain(query, key_in, value, mask, w_out):
    axes = ("tm", "pix")
    _, _, patches, feats = query.shape
    frames = lax.axis_size(axes)
    width, heads = patches // frames, feats // HDIM
    moved = [
        lax.all_to_all(a.reshape(frames, width, feats), axes, split_axis=0, concat_axis=0, tiled=True)
        .reshape(frames, width, heads, HDIM)
        for a in (query, key_in, value)
    ]
    block = jnp.arange(frames, dtype=jnp.int32) // (frames // mask.shape[0])
    allowed = mask[block][:, block] > 0
    scores = jnp.einsum("iphd,jphd->phij", moved[0], moved[1], preferred_element_type=jnp.float32) / HDIM**0.5
    scores = jnp.where(allowed, scores, -1e30)
    expo = jnp.exp(scores - jnp.max(scores, axis=-1, keepdims=True))
    total = jnp.transpose(jnp.sum(expo, axis=-1), (2, 0, 1))[..., None]
    summed = jnp.einsum("phij,jphd->iphd", expo.astype(jnp.bfloat16), moved[2], preferred_element_type=jnp.float32)
    attended = (summed / total).astype(jnp.bfloat16).reshape(frames, width, feats)
    projected = jnp.dot(attended, w_out, preferred_element_type=jnp.float32).astype(jnp.bfloat16)
    back = lax.all_to_all(projected, axes, split_axis=0, concat_axis=0, tiled=True)
    return back.reshape(query.shape)


def per_device(query, key_in, value, mask, w_out):
    axes = ("tm", "pix")
    _, _, patches, feats = query.shape
    frames = lax.axis_size(axes)
    if patches % (frames * SUB) != 0:
        return plain(query, key_in, value, mask, w_out)
    groups = patches // (frames * SUB)
    row = jnp.arange(frames * SUB, dtype=jnp.int32)
    bias = bias_of(mask, row // SUB, row % SUB, frames // mask.shape[0])
    parts = [a.reshape(groups, frames, SUB, feats) for a in (query, key_in, value)]
    packed = jnp.stack(parts, axis=1).transpose(2, 0, 1, 3, 4)
    qkv = lax.all_to_all(packed, axes, split_axis=0, concat_axis=0, tiled=True)
    out = attend(qkv, bias, w_out)
    back = lax.all_to_all(out, axes, split_axis=0, concat_axis=0, tiled=True)
    return back.transpose(1, 0, 2, 3).reshape(query.shape)


def solution(mesh):
    placed = P("tm", "pix", None, None)
    return jax.shard_map(
        per_device, mesh=mesh, in_specs=(placed, placed, placed, P(), P()), out_specs=placed, check_vma=False
    )
```

```python
import math

import jax
import jax.numpy as jnp
from jax import lax
from jax.experimental import pallas as pl
from jax.experimental.pallas import tpu as pltpu
from jax.sharding import PartitionSpec as P

HDIM = 72
LANES = 128
SUB = 8
HI = 4
AXES = ("tm", "pix")


def copies(pairs, sems):
    started = [pltpu.make_async_copy(src, dst, sems.at[i]) for i, (src, dst) in enumerate(pairs)]
    for c in started:
        c.start()
    for c in started:
        c.wait()


def mover(body, arrays, out_shapes, number, scalar):
    count = len(arrays)

    def kernel(z_ref, *refs):
        copies(body(z_ref[0], refs[:count], refs[count:-1]), refs[-1])

    return pl.pallas_call(
        kernel,
        grid_spec=pltpu.PrefetchScalarGridSpec(
            num_scalar_prefetch=1,
            in_specs=[pl.BlockSpec(memory_space=pl.ANY)] * count,
            out_specs=[pl.BlockSpec(memory_space=pltpu.VMEM)] * len(out_shapes),
            scratch_shapes=[pltpu.SemaphoreType.DMA((number,))],
        ),
        out_shape=[jax.ShapeDtypeStruct(s, jnp.bfloat16) for s in out_shapes],
        cost_estimate=pl.CostEstimate(flops=0, bytes_accessed=0, transcendentals=0),
    )(scalar.reshape(1), *arrays)


def attend_kernel(z_ref, *refs):
    slots, (bias_ref, w_ref, out_ref, acc_ref) = refs[:HI], refs[HI:]
    rows, feats = acc_ref.shape
    part = rows // HI
    scale = math.log2(math.e) / HDIM**0.5

    def load(which, start, stop):
        pieces = [s[:, 0, which, 0, :, start:stop].reshape(part, stop - start) for s in slots]
        return jnp.concatenate(pieces, axis=0)

    for head in range(feats // HDIM):
        low, high = head * HDIM, (head + 1) * HDIM
        start, stop = low // LANES * LANES, -(-high // LANES) * LANES
        lane = lax.broadcasted_iota(jnp.int32, (1, stop - start), 1) + start
        mine = (lane >= low) & (lane < high)
        q, k, v = (load(which, start, stop) for which in range(3))
        q = jnp.where(mine, q, jnp.zeros_like(q))
        scores = lax.dot_general(q, k, (((1,), (1,)), ((), ())), preferred_element_type=jnp.float32)
        scores = scores * scale + bias_ref[...]
        expo = jnp.exp2(scores - jnp.max(scores, axis=1, keepdims=True))
        share = 1.0 / jnp.sum(expo, axis=1, keepdims=True)
        summed = jnp.dot(expo.astype(jnp.bfloat16), v, preferred_element_type=jnp.float32)
        acc_ref[:, start:stop] = jnp.where(mine, summed * share, acc_ref[:, start:stop])
    attended = acc_ref[...].astype(jnp.bfloat16)
    projected = jnp.dot(attended, w_ref[...], preferred_element_type=jnp.float32).astype(jnp.bfloat16)
    for slot in range(HI):
        out_ref[:, slot, 0] = projected[slot * part : (slot + 1) * part].reshape(out_ref.shape[0], SUB, feats)


def attend(place, slots, bias, w_out):
    sources, _, _, groups, sub, feats = slots[0][0].shape
    rows = HI * sources * sub

    def spec(entry):
        if entry is None:
            return pl.BlockSpec((sources, 1, 3, 1, sub, feats), lambda g, z: (0, z[0], 0, g, 0, 0))
        return pl.BlockSpec((sources, 1, 3, 1, sub, feats), lambda g, z: (0, entry, 0, g, 0, 0))

    return pl.pallas_call(
        attend_kernel,
        grid_spec=pltpu.PrefetchScalarGridSpec(
            num_scalar_prefetch=1,
            grid=(groups,),
            in_specs=[spec(entry) for _, entry in slots]
            + [
                pl.BlockSpec((rows, rows), lambda g, z: (0, 0)),
                pl.BlockSpec((feats, feats), lambda g, z: (0, 0)),
            ],
            out_specs=pl.BlockSpec((sources, HI, 1, sub, feats), lambda g, z: (0, 0, g, 0, 0)),
            scratch_shapes=[pltpu.VMEM((rows, feats), jnp.float32)],
        ),
        out_shape=jax.ShapeDtypeStruct((sources, HI, groups, sub, feats), jnp.bfloat16),
        compiler_params=pltpu.CompilerParams(vmem_limit_bytes=48 * 2**20),
        cost_estimate=pl.CostEstimate(flops=0, bytes_accessed=0, transcendentals=0),
    )(place.reshape(1), *[a for a, _ in slots], bias, w_out)


def bias_of(mask, frame_of_row, patch_of_row, blen):
    block = frame_of_row // blen
    hot = (block[:, None] == jnp.arange(mask.shape[0], dtype=jnp.int32)).astype(jnp.float32)
    allowed = jnp.dot(jnp.dot(hot, mask.astype(jnp.float32)), hot.T) > 0.5
    return jnp.where(allowed & (patch_of_row[:, None] == patch_of_row[None, :]), 0.0, -1e30).astype(jnp.float32)


def plain(query, key_in, value, mask, w_out):
    _, _, patches, feats = query.shape
    frames = lax.axis_size(AXES)
    width, heads = patches // frames, feats // HDIM
    moved = [
        lax.all_to_all(a.reshape(frames, width, feats), AXES, split_axis=0, concat_axis=0, tiled=True)
        .reshape(frames, width, heads, HDIM)
        for a in (query, key_in, value)
    ]
    block = jnp.arange(frames, dtype=jnp.int32) // (frames // mask.shape[0])
    allowed = mask[block][:, block] > 0
    scores = jnp.einsum("iphd,jphd->phij", moved[0], moved[1], preferred_element_type=jnp.float32) / HDIM**0.5
    scores = jnp.where(allowed, scores, -1e30)
    expo = jnp.exp(scores - jnp.max(scores, axis=-1, keepdims=True))
    total = jnp.transpose(jnp.sum(expo, axis=-1), (2, 0, 1))[..., None]
    summed = jnp.einsum("phij,jphd->iphd", expo.astype(jnp.bfloat16), moved[2], preferred_element_type=jnp.float32)
    attended = (summed / total).astype(jnp.bfloat16).reshape(frames, width, feats)
    projected = jnp.dot(attended, w_out, preferred_element_type=jnp.float32).astype(jnp.bfloat16)
    back = lax.all_to_all(projected, AXES, split_axis=0, concat_axis=0, tiled=True)
    return back.reshape(query.shape)

def per_device(query, key_in, value, mask, w_out):
    _, _, patches, feats = query.shape
    n_tm, n_pix = lax.axis_size("tm"), lax.axis_size("pix")
    frames = n_tm * n_pix
    if n_pix % HI != 0 or patches != 4 * frames * SUB:
        return plain(query, key_in, value, mask, w_out)
    n_low = n_pix // HI
    plane = n_tm * n_low
    tall = 2 * SUB
    high = lax.axis_index("pix") // n_low
    teams = [[t * n_pix + z * n_low + x for t in range(n_tm) for x in range(n_low)] for z in range(HI)]
    order = [(p, t) for p in range(n_pix) for t in range(n_tm)]
    number = {device: i for i, device in enumerate(order)}
    tie = lax.optimization_barrier

    row = jnp.arange(HI * plane * SUB, dtype=jnp.int32)
    slot, source = row // (plane * SUB), row // SUB % plane
    frame = source // n_low * n_pix + (high ^ slot) * n_low + source % n_low
    bias = bias_of(mask, frame, row % SUB, frames // mask.shape[0])
    always = mask[0, 0] >= 0

    def region(f, *args):
        shapes = jax.eval_shape(f, *args)
        return lax.cond(always, f, lambda *_: jax.tree.map(lambda s: jnp.zeros(s.shape, s.dtype), shapes), *args)

    def along(a, k):
        pairs = [(number[(p, t)], number[((p // n_low ^ k) * n_low + p % n_low, t)]) for p, t in order]
        return lax.ppermute(a, ("pix", "tm"), pairs)

    def across(a):
        return lax.all_to_all(a, AXES, split_axis=0, concat_axis=0, tiled=True, axis_index_groups=teams)

    flat = [a.reshape(patches // tall, tall, feats) for a in (query, key_in, value)]
    piece = (plane, 3, tall, feats)
    whole = (plane, HI, 3, tall, feats)

    def cut(slots):
        def body(z, ins, outs):
            return [
                (a.at[pl.ds((z ^ k) * plane, plane)], out.at[:, t])
                for k, out in zip(slots, outs)
                for t, a in enumerate(ins)
            ]

        return lambda *flat: mover(body, flat, [piece] * len(slots), 3 * len(slots), high)

    far = cut((3, 2, 1))(*flat)
    far, flat = tie((far, flat))
    moved = [along(far[HI - 1 - k], k) for k in range(1, HI)]

    def pack(z, ins, outs):
        return [
            (a.at[pl.ds((HI + y) * plane, plane)], outs[0].at[:, y, t]) for y in range(HI) for t, a in enumerate(ins)
        ]

    def split(z, ins, outs):
        return [(ins[0].at[:, z ^ k], out) for k, out in enumerate(outs)]

    def start_second(*flat):
        [packed] = mover(pack, flat, [whole], 3 * HI, high)
        packed, flat = tie((packed, flat))
        return mover(split, [across(packed)], [piece] * HI, HI, high), cut((0,))(*flat)

    second, own = region(start_second, *flat)
    second, moved = tie((second, [*own, *moved]))
    second = [second[0]] + [along(second[k], k) for k in range(1, HI)]

    def gather(z, ins, outs):
        return [(a, outs[0].at[:, k]) for k, a in enumerate(ins)]

    def finish_first(moved, bias, w_out):
        [packed] = mover(gather, moved, [whole], HI, high)
        packed = across(packed).reshape(plane, HI, 3, 2, SUB, feats)
        return across(attend(high, [(packed, k) for k in range(HI)], bias, w_out))

    def finish_second(second, bias, w_out):
        second = [a.reshape(plane, 1, 3, 2, SUB, feats) for a in second]
        return across(attend(high, [(a, 0) for a in second], bias, w_out))

    def give_back(done):
        pieces = [done[:, k].reshape(plane * tall, feats) for k in range(HI)]
        return [pieces[0]] + [along(pieces[k], k) for k in range(1, HI)]

    done_first = region(finish_first, moved, bias, w_out)
    second, done_first = tie((second, done_first))
    back_first = give_back(done_first)
    done_second = region(finish_second, second, bias, w_out)
    back_first, done_second = tie((back_first, done_second))
    back_second = give_back(done_second)

    result = jnp.zeros((2 * HI, plane * tall, feats), jnp.bfloat16)
    for half, back in enumerate((back_first, back_second)):
        for k in range(HI):
            result = lax.dynamic_update_index_in_dim(result, back[k], half * HI + (high ^ k), 0)
    return result.reshape(query.shape)


def solution(mesh):
    placed = P("tm", "pix", None, None)
    return jax.shard_map(
        per_device, mesh=mesh, in_specs=(placed, placed, placed, P(), P()), out_specs=placed, check_vma=False
    )
```

```python
import math

import jax
import jax.numpy as jnp
from jax import lax
from jax.experimental import pallas as pl
from jax.experimental.pallas import tpu as pltpu
from jax.sharding import PartitionSpec as P

HDIM = 72
LANES = 128
SUB = 8
HI = 4
NEAR = (0, 2, 3, 1)
AXES = ("tm", "pix")


def mover(body, arrays, out_shapes, number, scalar):
    count, outs = len(arrays), len(out_shapes)

    def kernel(z_ref, *refs):
        sems, out_sems = refs[-2:]
        stages = refs[count + outs : count + 2 * outs]
        arriving, slot = [], 0
        for pairs in body(z_ref[0], refs[:count], stages):
            arriving.append([pltpu.make_async_copy(a, b, sems.at[slot + i]) for i, (a, b) in enumerate(pairs)])
            slot += len(pairs)
        leaving = [
            pltpu.make_async_copy(stages[i], refs[count + i], out_sems.at[i]) for i in range(outs)
        ]
        for copy in sum(arriving, []):
            copy.start()
        for copies, out in zip(arriving, leaving):
            for copy in copies:
                copy.wait()
            out.start()
        for out in leaving:
            out.wait()

    return pl.pallas_call(
        kernel,
        grid_spec=pltpu.PrefetchScalarGridSpec(
            num_scalar_prefetch=1,
            in_specs=[pl.BlockSpec(memory_space=pl.ANY)] * count,
            out_specs=[pl.BlockSpec(memory_space=pl.ANY)] * outs,
            scratch_shapes=[pltpu.VMEM(s, jnp.bfloat16) for s in out_shapes]
            + [pltpu.SemaphoreType.DMA((number,)), pltpu.SemaphoreType.DMA((outs,))],
        ),
        out_shape=[jax.ShapeDtypeStruct(s, jnp.bfloat16) for s in out_shapes],
        cost_estimate=pl.CostEstimate(flops=0, bytes_accessed=0, transcendentals=0),
    )(scalar.reshape(1), *arrays)


def attend_kernel(z_ref, *refs):
    slots, (bias_ref, w_hbm, out_ref, acc_ref, w_ref, w_sem) = refs[:HI], refs[HI:]
    rows, feats = acc_ref.shape
    part = rows // HI
    scale = math.log2(math.e) / HDIM**0.5
    fetch = pltpu.make_async_copy(w_hbm, w_ref, w_sem)

    @pl.when(pl.program_id(0) == 0)
    def _():
        fetch.start()

    def load(which, start, stop):
        pieces = [s[:, 0, which, 0, :, start:stop].reshape(part, stop - start) for s in slots]
        return jnp.concatenate(pieces, axis=0)

    heads = feats // HDIM

    def window(head):
        low, high = head * HDIM, (head + 1) * HDIM
        start, stop = low // LANES * LANES, -(-high // LANES) * LANES
        lane = lax.broadcasted_iota(jnp.int32, (1, stop - start), 1) + start
        return start, stop, (lane >= low) & (lane < high)

    def score(head):
        start, stop, mine = window(head)
        q, k = load(0, start, stop), load(1, start, stop)
        q = jnp.where(mine, q, jnp.zeros_like(q))
        return lax.dot_general(q, k, (((1,), (1,)), ((), ())), preferred_element_type=jnp.float32)

    def weigh(scores):
        scores = scores * scale + bias_ref[...]
        expo = jnp.exp2(scores - jnp.max(scores, axis=1, keepdims=True))
        return expo.astype(jnp.bfloat16), 1.0 / jnp.sum(expo, axis=1, keepdims=True)

    def blend(head, expo, share):
        start, stop, mine = window(head)
        summed = jnp.dot(expo, load(2, start, stop), preferred_element_type=jnp.float32)
        acc_ref[:, start:stop] = jnp.where(mine, (summed * share).astype(jnp.bfloat16), acc_ref[:, start:stop])

    scores = score(0)
    for head in range(heads):
        later = score(head + 1) if head + 1 < heads else None
        expo, share = weigh(scores)
        blend(head, expo, share)
        scores = later
    @pl.when(pl.program_id(0) == 0)
    def _():
        fetch.wait()

    projected = jnp.dot(acc_ref[...], w_ref[...], preferred_element_type=jnp.float32).astype(jnp.bfloat16)
    for slot in range(HI):
        out_ref[:, slot, 0] = projected[slot * part : (slot + 1) * part].reshape(out_ref.shape[0], SUB, feats)


def attend(place, slots, bias, w_out):
    sources, _, _, groups, sub, feats = slots[0][0].shape
    rows = HI * sources * sub

    def spec(entry):
        return pl.BlockSpec((sources, 1, 3, 1, sub, feats), lambda g, z: (0, entry, 0, g, 0, 0))

    return pl.pallas_call(
        attend_kernel,
        grid_spec=pltpu.PrefetchScalarGridSpec(
            num_scalar_prefetch=1,
            grid=(groups,),
            in_specs=[spec(entry) for _, entry in slots]
            + [pl.BlockSpec((rows, rows), lambda g, z: (0, 0)), pl.BlockSpec(memory_space=pl.ANY)],
            out_specs=pl.BlockSpec((sources, HI, 1, sub, feats), lambda g, z: (0, 0, g, 0, 0)),
            scratch_shapes=[
                pltpu.VMEM((rows, feats), jnp.bfloat16),
                pltpu.VMEM((feats, feats), jnp.bfloat16),
                pltpu.SemaphoreType.DMA,
            ],
        ),
        out_shape=jax.ShapeDtypeStruct((sources, HI, groups, sub, feats), jnp.bfloat16),
        compiler_params=pltpu.CompilerParams(vmem_limit_bytes=48 * 2**20),
        cost_estimate=pl.CostEstimate(flops=0, bytes_accessed=0, transcendentals=0),
    )(place.reshape(1), *[a for a, _ in slots], bias, w_out)


def bias_of(mask, frame_of_row, patch_of_row, blen):
    block = frame_of_row // blen
    hot = (block[:, None] == jnp.arange(mask.shape[0], dtype=jnp.int32)).astype(jnp.float32)
    allowed = jnp.dot(jnp.dot(hot, mask.astype(jnp.float32)), hot.T) > 0.5
    return jnp.where(allowed & (patch_of_row[:, None] == patch_of_row[None, :]), 0.0, -1e30).astype(jnp.float32)


def plain(query, key_in, value, mask, w_out):
    _, _, patches, feats = query.shape
    frames = lax.axis_size(AXES)
    width, heads = patches // frames, feats // HDIM
    moved = [
        lax.all_to_all(a.reshape(frames, width, feats), AXES, split_axis=0, concat_axis=0, tiled=True)
        .reshape(frames, width, heads, HDIM)
        for a in (query, key_in, value)
    ]
    block = jnp.arange(frames, dtype=jnp.int32) // (frames // mask.shape[0])
    allowed = mask[block][:, block] > 0
    scores = jnp.einsum("iphd,jphd->phij", moved[0], moved[1], preferred_element_type=jnp.float32) / HDIM**0.5
    scores = jnp.where(allowed, scores, -1e30)
    expo = jnp.exp(scores - jnp.max(scores, axis=-1, keepdims=True))
    total = jnp.transpose(jnp.sum(expo, axis=-1), (2, 0, 1))[..., None]
    summed = jnp.einsum("phij,jphd->iphd", expo.astype(jnp.bfloat16), moved[2], preferred_element_type=jnp.float32)
    attended = (summed / total).astype(jnp.bfloat16).reshape(frames, width, feats)
    projected = jnp.dot(attended, w_out, preferred_element_type=jnp.float32).astype(jnp.bfloat16)
    back = lax.all_to_all(projected, AXES, split_axis=0, concat_axis=0, tiled=True)
    return back.reshape(query.shape)

def per_device(query, key_in, value, mask, w_out):
    _, _, patches, feats = query.shape
    n_tm, n_pix = lax.axis_size("tm"), lax.axis_size("pix")
    frames = n_tm * n_pix
    if n_pix % HI != 0 or patches != 4 * frames * SUB:
        return plain(query, key_in, value, mask, w_out)
    n_low = n_pix // HI
    plane = n_tm * n_low
    tall = 2 * SUB
    high = lax.axis_index("pix") // n_low
    teams = [[t * n_pix + z * n_low + x for t in range(n_tm) for x in range(n_low)] for z in range(HI)]
    order = [(p, t) for p in range(n_pix) for t in range(n_tm)]
    number = {device: i for i, device in enumerate(order)}
    tie = lax.optimization_barrier

    row = jnp.arange(HI * plane * SUB, dtype=jnp.int32)
    slot, source = row // (plane * SUB), row // SUB % plane
    frame = source // n_low * n_pix + (high ^ sum(jnp.where(slot == s, k, 0) for s, k in enumerate(NEAR))) * n_low + source % n_low
    bias = bias_of(mask, frame, row % SUB, frames // mask.shape[0])
    always = mask[0, 0] >= 0

    def region(f, *args):
        shapes = jax.eval_shape(f, *args)
        return lax.cond(always, f, lambda *_: jax.tree.map(lambda s: jnp.zeros(s.shape, s.dtype), shapes), *args)

    def along(a, k):
        pairs = [(number[(p, t)], number[((p // n_low ^ k) * n_low + p % n_low, t)]) for p, t in order]
        return lax.ppermute(a, ("pix", "tm"), pairs)

    def across(a):
        return lax.all_to_all(a, AXES, split_axis=0, concat_axis=0, tiled=True, axis_index_groups=teams)

    flat = [a.reshape(patches // tall, tall, feats) for a in (query, key_in, value)]
    piece = (plane, 3, tall, feats)
    whole = (plane, HI, 3, tall, feats)

    def cut(slots):
        def body(z, ins, outs):
            return [
                [(a.at[pl.ds((z ^ k) * plane, plane)], out.at[:, t]) for t, a in enumerate(ins)]
                for k, out in zip(slots, outs)
            ]

        return lambda *flat: mover(body, flat, [piece] * len(slots), 3 * len(slots), high)

    far = cut(NEAR[1:])(*flat)
    far, flat = tie((far, flat))
    moved = [along(a, k) for a, k in zip(far, NEAR[1:])]

    def pack(z, ins, outs):
        return [
            [(a.at[pl.ds((HI + y) * plane, plane)], outs[0].at[:, y, t]) for y in range(HI) for t, a in enumerate(ins)]
        ]

    def split(z, ins, outs):
        return [[(ins[0].at[:, z ^ k], out)] for k, out in zip(NEAR, outs)]

    def start_second(*flat):
        [packed] = mover(pack, flat, [whole], 3 * HI, high)
        packed, flat = tie((packed, flat))
        return mover(split, [across(packed)], [piece] * HI, HI, high), cut((0,))(*flat)

    second, own = region(start_second, *flat)
    second, moved = tie((second, [*own, *moved]))
    second = [second[0], *[along(a, k) for a, k in zip(second[1:], NEAR[1:])]]

    def gather(z, ins, outs):
        return [[(a, outs[0].at[:, k]) for k, a in enumerate(ins)]]

    def finish_first(moved, bias, w_out):
        [packed] = mover(gather, moved, [whole], HI, high)
        packed = across(packed).reshape(plane, HI, 3, 2, SUB, feats)
        return across(attend(high, [(packed, k) for k in range(HI)], bias, w_out))

    def finish_second(second, bias, w_out):
        second = [a.reshape(plane, 1, 3, 2, SUB, feats) for a in second]
        return across(attend(high, [(a, 0) for a in second], bias, w_out))

    def give_back(done):
        pieces = [done[:, k].reshape(plane * tall, feats) for k in range(HI)]
        return [pieces[0], *[along(a, k) for a, k in zip(pieces[1:], NEAR[1:])]]

    done_first = region(finish_first, moved, bias, w_out)
    second[0], done_first = tie((second[0], done_first))
    back_first = give_back(done_first)
    done_second = region(finish_second, second, bias, w_out)
    back_first, done_second = tie((back_first, done_second))
    back_second = give_back(done_second)

    result = jnp.zeros((2 * HI, plane * tall, feats), jnp.bfloat16)
    for half, back in enumerate((back_first, back_second)):
        for k, piece in zip(NEAR, back):
            result = lax.dynamic_update_index_in_dim(result, piece, half * HI + (high ^ k), 0)
    return result.reshape(query.shape)


def solution(mesh):
    placed = P("tm", "pix", None, None)
    return jax.shard_map(
        per_device, mesh=mesh, in_specs=(placed, placed, placed, P(), P()), out_specs=placed, check_vma=False
    )
```

```python
import functools
import math

import jax
import jax.numpy as jnp
from jax import lax
from jax.experimental import pallas as pl
from jax.experimental.pallas import tpu as pltpu
from jax.sharding import PartitionSpec as P

HDIM = 72
LANES = 128
SUB = 8
HI = 4
NEAR = (0, 2, 3, 1)
AXES = ("tm", "pix")


def mover(body, arrays, out_shapes, number, scalar, stage_shapes=None, place=None, aliases=None):
    count, outs = len(arrays), len(out_shapes)
    stage_shapes = stage_shapes or out_shapes
    place = place or (lambda out_refs: out_refs)

    def kernel(z_ref, *refs):
        sems, out_sems = refs[-2:]
        stages, targets = refs[count + outs : -2], place(refs[count : count + outs])
        arriving, slot = [], 0
        for pairs in body(z_ref[0], refs[:count], stages):
            arriving.append([pltpu.make_async_copy(a, b, sems.at[slot + i]) for i, (a, b) in enumerate(pairs)])
            slot += len(pairs)
        leaving = [pltpu.make_async_copy(a, b, out_sems.at[i]) for i, (a, b) in enumerate(zip(stages, targets))]
        for copy in sum(arriving, []):
            copy.start()
        for copies, out in zip(arriving, leaving):
            for copy in copies:
                copy.wait()
            out.start()
        for out in leaving:
            out.wait()

    return pl.pallas_call(
        kernel,
        grid_spec=pltpu.PrefetchScalarGridSpec(
            num_scalar_prefetch=1,
            in_specs=[pl.BlockSpec(memory_space=pl.ANY)] * count,
            out_specs=[pl.BlockSpec(memory_space=pl.ANY)] * outs,
            scratch_shapes=[pltpu.VMEM(s, jnp.bfloat16) for s in stage_shapes]
            + [pltpu.SemaphoreType.DMA((number,)), pltpu.SemaphoreType.DMA((len(stage_shapes),))],
        ),
        out_shape=[jax.ShapeDtypeStruct(s, jnp.bfloat16) for s in out_shapes],
        input_output_aliases=aliases or {},
        cost_estimate=pl.CostEstimate(flops=0, bytes_accessed=0, transcendentals=0),
    )(scalar.reshape(1), *arrays)


def attend_kernel(by_frame, z_ref, *refs):
    slots, (bias_ref, w_hbm, out_ref, acc_ref, w_ref, w_sem) = refs[:HI], refs[HI:]
    rows, feats = acc_ref.shape
    part = rows // HI
    scale = math.log2(math.e) / HDIM**0.5
    fetch = pltpu.make_async_copy(w_hbm, w_ref, w_sem)

    @pl.when(pl.program_id(0) == 0)
    def _():
        fetch.start()

    def load(which, start, stop):
        pieces = [s[:, 0, which, 0, :, start:stop].reshape(part, stop - start) for s in slots]
        return jnp.concatenate(pieces, axis=0)

    heads = feats // HDIM

    def window(head):
        low, high = head * HDIM, (head + 1) * HDIM
        start, stop = low // LANES * LANES, -(-high // LANES) * LANES
        lane = lax.broadcasted_iota(jnp.int32, (1, stop - start), 1) + start
        return start, stop, (lane >= low) & (lane < high)

    def score(head):
        start, stop, mine = window(head)
        q, k = load(0, start, stop), load(1, start, stop)
        q = jnp.where(mine, q, jnp.zeros_like(q))
        return lax.dot_general(q, k, (((1,), (1,)), ((), ())), preferred_element_type=jnp.float32)

    def weigh(scores):
        scores = scores * scale + bias_ref[...]
        expo = jnp.exp2(scores - jnp.max(scores, axis=1, keepdims=True))
        return expo.astype(jnp.bfloat16), 1.0 / jnp.sum(expo, axis=1, keepdims=True)

    def blend(head, expo, share):
        start, stop, mine = window(head)
        summed = jnp.dot(expo, load(2, start, stop), preferred_element_type=jnp.float32)
        acc_ref[:, start:stop] = jnp.where(mine, (summed * share).astype(jnp.bfloat16), acc_ref[:, start:stop])

    scores = score(0)
    for head in range(heads):
        later = score(head + 1) if head + 1 < heads else None
        expo, share = weigh(scores)
        blend(head, expo, share)
        scores = later
    @pl.when(pl.program_id(0) == 0)
    def _():
        fetch.wait()

    projected = jnp.dot(acc_ref[...], w_ref[...], preferred_element_type=jnp.float32).astype(jnp.bfloat16)
    for slot, k in enumerate(NEAR):
        own = projected[slot * part : (slot + 1) * part]
        if by_frame:
            out_ref[:, z_ref[0] ^ k, :, 0] = own.reshape(out_ref.shape[0], out_ref.shape[2], SUB, feats)
        else:
            out_ref[:, slot, 0] = own.reshape(out_ref.shape[0], SUB, feats)


def attend(place, slots, bias, w_out, outer=None):
    sources, _, _, groups, sub, feats = slots[0][0].shape
    rows = HI * sources * sub

    shape = (sources, HI) if outer is None else (outer, HI, sources // outer)
    zeros = (0,) * len(shape)

    def spec(entry):
        return pl.BlockSpec((sources, 1, 3, 1, sub, feats), lambda g, z: (0, entry, 0, g, 0, 0))

    return pl.pallas_call(
        functools.partial(attend_kernel, outer is not None),
        grid_spec=pltpu.PrefetchScalarGridSpec(
            num_scalar_prefetch=1,
            grid=(groups,),
            in_specs=[spec(entry) for _, entry in slots]
            + [pl.BlockSpec((rows, rows), lambda g, z: (0, 0)), pl.BlockSpec(memory_space=pl.ANY)],
            out_specs=pl.BlockSpec((*shape, 1, sub, feats), lambda g, z: (*zeros, g, 0, 0)),
            scratch_shapes=[
                pltpu.VMEM((rows, feats), jnp.bfloat16),
                pltpu.VMEM((feats, feats), jnp.bfloat16),
                pltpu.SemaphoreType.DMA,
            ],
        ),
        out_shape=jax.ShapeDtypeStruct((*shape, groups, sub, feats), jnp.bfloat16),
        compiler_params=pltpu.CompilerParams(vmem_limit_bytes=48 * 2**20),
        cost_estimate=pl.CostEstimate(flops=0, bytes_accessed=0, transcendentals=0),
    )(place.reshape(1), *[a for a, _ in slots], bias, w_out)


def bias_of(mask, frame_of_row, patch_of_row, blen):
    block = frame_of_row // blen
    hot = (block[:, None] == jnp.arange(mask.shape[0], dtype=jnp.int32)).astype(jnp.float32)
    allowed = jnp.dot(jnp.dot(hot, mask.astype(jnp.float32)), hot.T) > 0.5
    return jnp.where(allowed & (patch_of_row[:, None] == patch_of_row[None, :]), 0.0, -1e30).astype(jnp.float32)


def plain(query, key_in, value, mask, w_out):
    _, _, patches, feats = query.shape
    frames = lax.axis_size(AXES)
    width, heads = patches // frames, feats // HDIM
    moved = [
        lax.all_to_all(a.reshape(frames, width, feats), AXES, split_axis=0, concat_axis=0, tiled=True)
        .reshape(frames, width, heads, HDIM)
        for a in (query, key_in, value)
    ]
    block = jnp.arange(frames, dtype=jnp.int32) // (frames // mask.shape[0])
    allowed = mask[block][:, block] > 0
    scores = jnp.einsum("iphd,jphd->phij", moved[0], moved[1], preferred_element_type=jnp.float32) / HDIM**0.5
    scores = jnp.where(allowed, scores, -1e30)
    expo = jnp.exp(scores - jnp.max(scores, axis=-1, keepdims=True))
    total = jnp.transpose(jnp.sum(expo, axis=-1), (2, 0, 1))[..., None]
    summed = jnp.einsum("phij,jphd->iphd", expo.astype(jnp.bfloat16), moved[2], preferred_element_type=jnp.float32)
    attended = (summed / total).astype(jnp.bfloat16).reshape(frames, width, feats)
    projected = jnp.dot(attended, w_out, preferred_element_type=jnp.float32).astype(jnp.bfloat16)
    back = lax.all_to_all(projected, AXES, split_axis=0, concat_axis=0, tiled=True)
    return back.reshape(query.shape)

def per_device(query, key_in, value, mask, w_out):
    _, _, patches, feats = query.shape
    n_tm, n_pix = lax.axis_size("tm"), lax.axis_size("pix")
    frames = n_tm * n_pix
    if n_pix % HI != 0 or patches != 4 * frames * SUB:
        return plain(query, key_in, value, mask, w_out)
    n_low = n_pix // HI
    plane = n_tm * n_low
    tall = 2 * SUB
    high = lax.axis_index("pix") // n_low
    teams = [[t * n_pix + z * n_low + x for t in range(n_tm) for x in range(n_low)] for z in range(HI)]
    order = [(p, t) for p in range(n_pix) for t in range(n_tm)]
    number = {device: i for i, device in enumerate(order)}
    tie = lax.optimization_barrier

    row = jnp.arange(HI * plane * SUB, dtype=jnp.int32)
    slot, source = row // (plane * SUB), row // SUB % plane
    frame = source // n_low * n_pix + (high ^ sum(jnp.where(slot == s, k, 0) for s, k in enumerate(NEAR))) * n_low + source % n_low
    blen = frames // mask.shape[0]
    always = mask[0, 0] >= 0

    def region(f, *args):
        shapes = jax.eval_shape(f, *args)
        return lax.cond(always, f, lambda *_: jax.tree.map(lambda s: jnp.zeros(s.shape, s.dtype), shapes), *args)

    def along(a, k):
        pairs = [(number[(p, t)], number[((p // n_low ^ k) * n_low + p % n_low, t)]) for p, t in order]
        return lax.ppermute(a, ("pix", "tm"), pairs)

    def across(a):
        return lax.all_to_all(a, AXES, split_axis=0, concat_axis=0, tiled=True, axis_index_groups=teams)

    flat = [a.reshape(patches // tall, tall, feats) for a in (query, key_in, value)]
    piece = (plane, 3, tall, feats)
    whole = (plane, HI, 3, tall, feats)

    def cut(slots):
        def body(z, ins, outs):
            return [
                [(a.at[pl.ds((z ^ k) * plane, plane)], out.at[:, t]) for t, a in enumerate(ins)]
                for k, out in zip(slots, outs)
            ]

        return lambda *flat: mover(body, flat, [piece] * len(slots), 3 * len(slots), high)

    far = cut(NEAR[1:])(*flat)
    far, flat = tie((far, flat))
    moved = [along(a, k) for a, k in zip(far, NEAR[1:])]

    def pack(z, ins, outs):
        return [
            [(a.at[1, :, y], outs[0].at[:, :, y, t]) for y in range(HI) for t, a in enumerate(ins)]
        ]

    def split(z, ins, outs):
        return [[(ins[0].at[:, z ^ k], out)] for k, out in zip(NEAR, outs)]

    def start_second(*flat):
        owned = [a.reshape(2, n_tm, HI, n_low, tall, feats) for a in flat]
        [packed] = mover(pack, owned, [(n_tm, n_low, *whole[1:])], 3 * HI, high)
        packed, flat = tie((packed.reshape(whole), flat))
        bias = bias_of(mask, frame, row % SUB, blen)
        return mover(split, [across(packed)], [piece] * HI, HI, high), cut((0,))(*flat), bias

    second, own, bias = region(start_second, *flat)
    late = NEAR.index(3)
    slots = [s for s in range(HI) if s != late]

    def each(z, ins, stages):
        return [[(a, stage)] for a, stage in zip(ins, stages)]

    def early_place(outs):
        return [outs[0].at[:, s] for s in slots]

    early = [[*own, *moved][s] for s in slots]
    packed = mover(each, early, [whole], HI - 1, high, [piece] * (HI - 1), early_place)
    second, packed, last = tie((second, packed, moved[late - 1]))
    second = [second[0], *[along(a, k) for a, k in zip(second[1:], NEAR[1:])]]
    [packed] = mover(each, [last, *packed], [whole], 1, high, [piece], lambda outs: [outs[0].at[:, late]], {2: 0})

    def finish_first(packed, bias, w_out):
        packed = across(packed).reshape(plane, HI, 3, 2, SUB, feats)
        return across(attend(high, [(packed, k) for k in range(HI)], bias, w_out))

    def finish_second(second, bias, w_out):
        second = [a.reshape(plane, 1, 3, 2, SUB, feats) for a in second]
        out = attend(high, [(a, 0) for a in second], bias, w_out, n_tm)
        return lax.all_to_all(out.reshape(frames, tall, feats), AXES, split_axis=0, concat_axis=0, tiled=True)

    def give_back(done):
        pieces = [done[:, k].reshape(plane * tall, feats) for k in range(HI)]
        return [pieces[0], *[along(a, k) for a, k in zip(pieces[1:], NEAR[1:])]]

    done_first = region(finish_first, packed, bias, w_out)
    second[0], done_first = tie((second[0], done_first))
    back_first = give_back(done_first)
    done_second = region(finish_second, second, bias, w_out)
    back_first, done_second = tie((back_first, done_second))
    result = jnp.zeros((2 * HI, plane * tall, feats), jnp.bfloat16)
    for k, piece in zip(NEAR, back_first):
        result = lax.dynamic_update_index_in_dim(result, piece, high ^ k, 0)
    result = lax.dynamic_update_slice(result, done_second.reshape(HI, plane * tall, feats), (HI, 0, 0))
    return result.reshape(query.shape)


def solution(mesh):
    placed = P("tm", "pix", None, None)
    return jax.shard_map(
        per_device, mesh=mesh, in_specs=(placed, placed, placed, P(), P()), out_specs=placed, check_vma=False
    )
```

```python
import functools
import math

import jax
import jax.numpy as jnp
from jax import lax
from jax.experimental import pallas as pl
from jax.experimental.pallas import tpu as pltpu
from jax.sharding import PartitionSpec as P

HDIM = 72
LANES = 128
SUB = 8
HI = 4
NEAR = (0, 3, 2, 1)
AXES = ("tm", "pix")


def mover(body, arrays, out_shapes, number, scalar, stage_shapes=None, place=None, aliases=None):
    count, outs = len(arrays), len(out_shapes)
    stage_shapes = stage_shapes or out_shapes
    place = place or (lambda out_refs: out_refs)

    def kernel(z_ref, *refs):
        sems, out_sems = refs[-2:]
        stages, targets = refs[count + outs : -2], place(refs[count : count + outs])
        arriving, slot = [], 0
        for pairs in body(z_ref[0], refs[:count], stages):
            arriving.append([pltpu.make_async_copy(a, b, sems.at[slot + i]) for i, (a, b) in enumerate(pairs)])
            slot += len(pairs)
        leaving = [pltpu.make_async_copy(a, b, out_sems.at[i]) for i, (a, b) in enumerate(zip(stages, targets))]
        for copy in sum(arriving, []):
            copy.start()
        for copies, out in zip(arriving, leaving):
            for copy in copies:
                copy.wait()
            out.start()
        for out in leaving:
            out.wait()

    return pl.pallas_call(
        kernel,
        grid_spec=pltpu.PrefetchScalarGridSpec(
            num_scalar_prefetch=1,
            in_specs=[pl.BlockSpec(memory_space=pl.ANY)] * count,
            out_specs=[pl.BlockSpec(memory_space=pl.ANY)] * outs,
            scratch_shapes=[pltpu.VMEM(s, jnp.bfloat16) for s in stage_shapes]
            + [pltpu.SemaphoreType.DMA((number,)), pltpu.SemaphoreType.DMA((len(stage_shapes),))],
        ),
        out_shape=[jax.ShapeDtypeStruct(s, jnp.bfloat16) for s in out_shapes],
        input_output_aliases=aliases or {},
        cost_estimate=pl.CostEstimate(flops=0, bytes_accessed=0, transcendentals=0),
    )(scalar.reshape(1), *arrays)


def attend_kernel(by_frame, z_ref, *refs):
    slots, (bias_ref, w_hbm, out_ref, acc_ref, w_ref, w_sem) = refs[:HI], refs[HI:]
    rows, feats = acc_ref.shape
    part = rows // HI
    scale = math.log2(math.e) / HDIM**0.5
    fetch = pltpu.make_async_copy(w_hbm, w_ref, w_sem)

    @pl.when(pl.program_id(0) == 0)
    def _():
        fetch.start()

    def load(which, start, stop):
        pieces = [s[:, 0, which, 0, :, start:stop].reshape(part, stop - start) for s in slots]
        return jnp.concatenate(pieces, axis=0)

    heads = feats // HDIM

    def window(head):
        low, high = head * HDIM, (head + 1) * HDIM
        start, stop = low // LANES * LANES, -(-high // LANES) * LANES
        lane = lax.broadcasted_iota(jnp.int32, (1, stop - start), 1) + start
        return start, stop, (lane >= low) & (lane < high)

    def score(head):
        start, stop, mine = window(head)
        q, k = load(0, start, stop), load(1, start, stop)
        q = jnp.where(mine, q, jnp.zeros_like(q))
        return lax.dot_general(q, k, (((1,), (1,)), ((), ())), preferred_element_type=jnp.float32)

    def weigh(scores):
        scores = scores * scale + bias_ref[...]
        expo = jnp.exp2(scores - jnp.max(scores, axis=1, keepdims=True))
        return expo.astype(jnp.bfloat16), 1.0 / jnp.sum(expo, axis=1, keepdims=True)

    def blend(head, expo, share):
        start, stop, mine = window(head)
        summed = jnp.dot(expo, load(2, start, stop), preferred_element_type=jnp.float32)
        acc_ref[:, start:stop] = jnp.where(mine, (summed * share).astype(jnp.bfloat16), acc_ref[:, start:stop])

    scores = score(0)
    for head in range(heads):
        later = score(head + 1) if head + 1 < heads else None
        expo, share = weigh(scores)
        blend(head, expo, share)
        scores = later
    @pl.when(pl.program_id(0) == 0)
    def _():
        fetch.wait()

    projected = jnp.dot(acc_ref[...], w_ref[...], preferred_element_type=jnp.float32).astype(jnp.bfloat16)
    for slot, k in enumerate(NEAR):
        own = projected[slot * part : (slot + 1) * part]
        if by_frame:
            out_ref[:, z_ref[0] ^ k, :, 0] = own.reshape(out_ref.shape[0], out_ref.shape[2], SUB, feats)
        else:
            out_ref[:, slot, 0] = own.reshape(out_ref.shape[0], SUB, feats)


def attend(place, slots, bias, w_out, outer=None):
    sources, _, _, groups, sub, feats = slots[0][0].shape
    rows = HI * sources * sub

    shape = (sources, HI) if outer is None else (outer, HI, sources // outer)
    zeros = (0,) * len(shape)

    def spec(entry):
        return pl.BlockSpec((sources, 1, 3, 1, sub, feats), lambda g, z: (0, entry, 0, g, 0, 0))

    return pl.pallas_call(
        functools.partial(attend_kernel, outer is not None),
        grid_spec=pltpu.PrefetchScalarGridSpec(
            num_scalar_prefetch=1,
            grid=(groups,),
            in_specs=[spec(entry) for _, entry in slots]
            + [pl.BlockSpec((rows, rows), lambda g, z: (0, 0)), pl.BlockSpec(memory_space=pl.ANY)],
            out_specs=pl.BlockSpec((*shape, 1, sub, feats), lambda g, z: (*zeros, g, 0, 0)),
            scratch_shapes=[
                pltpu.VMEM((rows, feats), jnp.bfloat16),
                pltpu.VMEM((feats, feats), jnp.bfloat16),
                pltpu.SemaphoreType.DMA,
            ],
        ),
        out_shape=jax.ShapeDtypeStruct((*shape, groups, sub, feats), jnp.bfloat16),
        compiler_params=pltpu.CompilerParams(vmem_limit_bytes=48 * 2**20),
        cost_estimate=pl.CostEstimate(flops=0, bytes_accessed=0, transcendentals=0),
    )(place.reshape(1), *[a for a, _ in slots], bias, w_out)


def bias_of(mask, frame_of_row, patch_of_row, blen):
    block = frame_of_row // blen
    hot = (block[:, None] == jnp.arange(mask.shape[0], dtype=jnp.int32)).astype(jnp.float32)
    allowed = jnp.dot(jnp.dot(hot, mask.astype(jnp.float32)), hot.T) > 0.5
    return jnp.where(allowed & (patch_of_row[:, None] == patch_of_row[None, :]), 0.0, -1e30).astype(jnp.float32)


def plain(query, key_in, value, mask, w_out):
    _, _, patches, feats = query.shape
    frames = lax.axis_size(AXES)
    width, heads = patches // frames, feats // HDIM
    moved = [
        lax.all_to_all(a.reshape(frames, width, feats), AXES, split_axis=0, concat_axis=0, tiled=True)
        .reshape(frames, width, heads, HDIM)
        for a in (query, key_in, value)
    ]
    block = jnp.arange(frames, dtype=jnp.int32) // (frames // mask.shape[0])
    allowed = mask[block][:, block] > 0
    scores = jnp.einsum("iphd,jphd->phij", moved[0], moved[1], preferred_element_type=jnp.float32) / HDIM**0.5
    scores = jnp.where(allowed, scores, -1e30)
    expo = jnp.exp(scores - jnp.max(scores, axis=-1, keepdims=True))
    total = jnp.transpose(jnp.sum(expo, axis=-1), (2, 0, 1))[..., None]
    summed = jnp.einsum("phij,jphd->iphd", expo.astype(jnp.bfloat16), moved[2], preferred_element_type=jnp.float32)
    attended = (summed / total).astype(jnp.bfloat16).reshape(frames, width, feats)
    projected = jnp.dot(attended, w_out, preferred_element_type=jnp.float32).astype(jnp.bfloat16)
    back = lax.all_to_all(projected, AXES, split_axis=0, concat_axis=0, tiled=True)
    return back.reshape(query.shape)

def per_device(query, key_in, value, mask, w_out):
    _, _, patches, feats = query.shape
    n_tm, n_pix = lax.axis_size("tm"), lax.axis_size("pix")
    frames = n_tm * n_pix
    if n_pix % HI != 0 or patches != 4 * frames * SUB:
        return plain(query, key_in, value, mask, w_out)
    n_low = n_pix // HI
    plane = n_tm * n_low
    tall = 2 * SUB
    high = lax.axis_index("pix") // n_low
    teams = [[t * n_pix + z * n_low + x for t in range(n_tm) for x in range(n_low)] for z in range(HI)]
    order = [(p, t) for p in range(n_pix) for t in range(n_tm)]
    number = {device: i for i, device in enumerate(order)}
    tie = lax.optimization_barrier

    row = jnp.arange(HI * plane * SUB, dtype=jnp.int32)
    slot, source = row // (plane * SUB), row // SUB % plane
    frame = source // n_low * n_pix + (high ^ sum(jnp.where(slot == s, k, 0) for s, k in enumerate(NEAR))) * n_low + source % n_low
    blen = frames // mask.shape[0]
    always = mask[0, 0] >= 0

    def region(f, *args):
        shapes = jax.eval_shape(f, *args)
        return lax.cond(always, f, lambda *_: jax.tree.map(lambda s: jnp.zeros(s.shape, s.dtype), shapes), *args)

    def along(a, k):
        pairs = [(number[(p, t)], number[((p // n_low ^ k) * n_low + p % n_low, t)]) for p, t in order]
        return lax.ppermute(a, ("pix", "tm"), pairs)

    def across(a):
        return lax.all_to_all(a, AXES, split_axis=0, concat_axis=0, tiled=True, axis_index_groups=teams)

    flat = [a.reshape(patches // tall, tall, feats) for a in (query, key_in, value)]
    piece = (plane, 3, tall, feats)
    whole = (plane, HI, 3, tall, feats)

    def cut(slots):
        def body(z, ins, outs):
            return [
                [(a.at[pl.ds((z ^ k) * plane, plane)], out.at[:, t]) for t, a in enumerate(ins)]
                for k, out in zip(slots, outs)
            ]

        return lambda *flat: mover(body, flat, [piece] * len(slots), 3 * len(slots), high)

    far = cut(NEAR[1:])(*flat)
    far, flat = tie((far, flat))
    moved = [along(a, k) for a, k in zip(far, NEAR[1:])]

    def pack(z, ins, outs):
        return [
            [(a.at[1, :, y], outs[0].at[:, :, y, t]) for y in range(HI) for t, a in enumerate(ins)]
        ]

    def split(z, ins, outs):
        return [[(ins[0].at[:, z ^ k], out)] for k, out in zip(NEAR, outs)]

    def start_second(*flat):
        owned = [a.reshape(2, n_tm, HI, n_low, tall, feats) for a in flat]
        [packed] = mover(pack, owned, [(n_tm, n_low, *whole[1:])], 3 * HI, high)
        packed, flat = tie((packed.reshape(whole), flat))
        bias = bias_of(mask, frame, row % SUB, blen)
        return mover(split, [across(packed)], [piece] * HI, HI, high), cut((0,))(*flat), bias

    second, own, bias = region(start_second, *flat)
    late = NEAR.index(2)
    slots = [s for s in range(HI) if s != late]

    def each(z, ins, stages):
        return [[(a, stage)] for a, stage in zip(ins, stages)]

    def early_place(outs):
        return [outs[0].at[:, s] for s in slots]

    early = [[*own, *moved][s] for s in slots]
    packed = mover(each, early, [whole], HI - 1, high, [piece] * (HI - 1), early_place)
    second, packed, last = tie((second, packed, moved[late - 1]))
    second = [second[0], *[along(a, k) for a, k in zip(second[1:], NEAR[1:])]]
    [packed] = mover(each, [last, *packed], [whole], 1, high, [piece], lambda outs: [outs[0].at[:, late]], {2: 0})

    def finish_first(packed, bias, w_out):
        packed = across(packed).reshape(plane, HI, 3, 2, SUB, feats)
        return across(attend(high, [(packed, k) for k in range(HI)], bias, w_out))

    def finish_second(second, bias, w_out):
        second = [a.reshape(plane, 1, 3, 2, SUB, feats) for a in second]
        out = attend(high, [(a, 0) for a in second], bias, w_out, n_tm)
        return lax.all_to_all(out.reshape(frames, tall, feats), AXES, split_axis=0, concat_axis=0, tiled=True)

    def give_back(done):
        pieces = [done[:, k].reshape(plane * tall, feats) for k in range(HI)]
        return [pieces[0], *[along(a, k) for a, k in zip(pieces[1:], NEAR[1:])]]

    done_first = region(finish_first, packed, bias, w_out)
    second[0], done_first = tie((second[0], done_first))
    back_first = give_back(done_first)
    done_second = region(finish_second, second, bias, w_out)
    back_first, done_second = tie((back_first, done_second))
    result = jnp.zeros((2 * HI, plane * tall, feats), jnp.bfloat16)
    for k, piece in zip(NEAR, back_first):
        result = lax.dynamic_update_index_in_dim(result, piece, high ^ k, 0)
    result = lax.dynamic_update_slice(result, done_second.reshape(HI, plane * tall, feats), (HI, 0, 0))
    return result.reshape(query.shape)


def solution(mesh):
    placed = P("tm", "pix", None, None)
    return jax.shard_map(
        per_device, mesh=mesh, in_specs=(placed, placed, placed, P(), P()), out_specs=placed, check_vma=False
    )
```

```python
import functools
import math

import jax
import jax.numpy as jnp
from jax import lax
from jax.experimental import pallas as pl
from jax.experimental.pallas import tpu as pltpu
from jax.sharding import PartitionSpec as P

HDIM = 72
LANES = 128
SUB = 8
HI = 4
NEAR = (0, 3, 2, 1)
AXES = ("tm", "pix")


def mover(body, arrays, out_shapes, number, scalar, stage_shapes=None, place=None, aliases=None):
    count, outs = len(arrays), len(out_shapes)
    stage_shapes = stage_shapes or out_shapes
    place = place or (lambda out_refs: out_refs)

    def kernel(z_ref, *refs):
        sems, out_sems = refs[-2:]
        stages, targets = refs[count + outs : -2], place(refs[count : count + outs])
        arriving, slot = [], 0
        for pairs in body(z_ref[0], refs[:count], stages):
            arriving.append([pltpu.make_async_copy(a, b, sems.at[slot + i]) for i, (a, b) in enumerate(pairs)])
            slot += len(pairs)
        leaving = [pltpu.make_async_copy(a, b, out_sems.at[i]) for i, (a, b) in enumerate(zip(stages, targets))]
        for copy in sum(arriving, []):
            copy.start()
        for copies, out in zip(arriving, leaving):
            for copy in copies:
                copy.wait()
            out.start()
        for out in leaving:
            out.wait()

    return pl.pallas_call(
        kernel,
        grid_spec=pltpu.PrefetchScalarGridSpec(
            num_scalar_prefetch=1,
            in_specs=[pl.BlockSpec(memory_space=pl.ANY)] * count,
            out_specs=[pl.BlockSpec(memory_space=pl.ANY)] * outs,
            scratch_shapes=[pltpu.VMEM(s, jnp.bfloat16) for s in stage_shapes]
            + [pltpu.SemaphoreType.DMA((number,)), pltpu.SemaphoreType.DMA((len(stage_shapes),))],
        ),
        out_shape=[jax.ShapeDtypeStruct(s, jnp.bfloat16) for s in out_shapes],
        input_output_aliases=aliases or {},
        cost_estimate=pl.CostEstimate(flops=0, bytes_accessed=0, transcendentals=0),
    )(scalar.reshape(1), *arrays)


def attend_kernel(by_frame, z_ref, *refs):
    slots, (bias_ref, w_hbm, out_ref, acc_ref, w_ref, w_sem) = refs[:HI], refs[HI:]
    rows, feats = acc_ref.shape
    part = rows // HI
    scale = math.log2(math.e) / HDIM**0.5
    fetch = pltpu.make_async_copy(w_hbm, w_ref, w_sem)

    @pl.when(pl.program_id(0) == 0)
    def _():
        fetch.start()

    def load(which, start, stop):
        pieces = [s[:, 0, which, 0, :, start:stop].reshape(part, stop - start) for s in slots]
        return jnp.concatenate(pieces, axis=0)

    heads = feats // HDIM

    def window(head):
        low, high = head * HDIM, (head + 1) * HDIM
        start, stop = low // LANES * LANES, -(-high // LANES) * LANES
        lane = lax.broadcasted_iota(jnp.int32, (1, stop - start), 1) + start
        return start, stop, (lane >= low) & (lane < high)

    def score(head):
        start, stop, mine = window(head)
        q, k = load(0, start, stop), load(1, start, stop)
        q = jnp.where(mine, q, jnp.zeros_like(q))
        return lax.dot_general(q, k, (((1,), (1,)), ((), ())), preferred_element_type=jnp.float32)

    def weigh(scores):
        scores = scores * scale + bias_ref[...]
        expo = jnp.exp2(scores - jnp.max(scores, axis=1, keepdims=True))
        return expo.astype(jnp.bfloat16), 1.0 / jnp.sum(expo, axis=1, keepdims=True)

    def blend(head, expo, share):
        start, stop, mine = window(head)
        summed = jnp.dot(expo, load(2, start, stop), preferred_element_type=jnp.float32)
        acc_ref[:, start:stop] = jnp.where(mine, (summed * share).astype(jnp.bfloat16), acc_ref[:, start:stop])

    scores = score(0)
    for head in range(heads):
        later = score(head + 1) if head + 1 < heads else None
        expo, share = weigh(scores)
        blend(head, expo, share)
        scores = later
    @pl.when(pl.program_id(0) == 0)
    def _():
        fetch.wait()

    projected = jnp.dot(acc_ref[...], w_ref[...], preferred_element_type=jnp.float32).astype(jnp.bfloat16)
    for slot, k in enumerate(NEAR):
        own = projected[slot * part : (slot + 1) * part]
        if by_frame:
            out_ref[:, z_ref[0] ^ k, :, 0] = own.reshape(out_ref.shape[0], out_ref.shape[2], SUB, feats)
        else:
            out_ref[:, slot, 0] = own.reshape(out_ref.shape[0], SUB, feats)


def attend(place, slots, bias, w_out, outer=None):
    sources, _, _, groups, sub, feats = slots[0][0].shape
    rows = HI * sources * sub

    shape = (sources, HI) if outer is None else (outer, HI, sources // outer)
    zeros = (0,) * len(shape)

    def spec(entry):
        return pl.BlockSpec((sources, 1, 3, 1, sub, feats), lambda g, z: (0, entry, 0, g, 0, 0))

    return pl.pallas_call(
        functools.partial(attend_kernel, outer is not None),
        grid_spec=pltpu.PrefetchScalarGridSpec(
            num_scalar_prefetch=1,
            grid=(groups,),
            in_specs=[spec(entry) for _, entry in slots]
            + [pl.BlockSpec((rows, rows), lambda g, z: (0, 0)), pl.BlockSpec(memory_space=pl.ANY)],
            out_specs=pl.BlockSpec((*shape, 1, sub, feats), lambda g, z: (*zeros, g, 0, 0)),
            scratch_shapes=[
                pltpu.VMEM((rows, feats), jnp.bfloat16),
                pltpu.VMEM((feats, feats), jnp.bfloat16),
                pltpu.SemaphoreType.DMA,
            ],
        ),
        out_shape=jax.ShapeDtypeStruct((*shape, groups, sub, feats), jnp.bfloat16),
        compiler_params=pltpu.CompilerParams(vmem_limit_bytes=48 * 2**20),
        cost_estimate=pl.CostEstimate(flops=0, bytes_accessed=0, transcendentals=0),
    )(place.reshape(1), *[a for a, _ in slots], bias, w_out)


def bias_of(mask, frame_of_row, patch_of_row, blen):
    block = frame_of_row // blen
    hot = (block[:, None] == jnp.arange(mask.shape[0], dtype=jnp.int32)).astype(jnp.float32)
    allowed = jnp.dot(jnp.dot(hot, mask.astype(jnp.float32)), hot.T) > 0.5
    return jnp.where(allowed & (patch_of_row[:, None] == patch_of_row[None, :]), 0.0, -1e30).astype(jnp.float32)


def plain(query, key_in, value, mask, w_out):
    _, _, patches, feats = query.shape
    frames = lax.axis_size(AXES)
    width, heads = patches // frames, feats // HDIM
    moved = [
        lax.all_to_all(a.reshape(frames, width, feats), AXES, split_axis=0, concat_axis=0, tiled=True)
        .reshape(frames, width, heads, HDIM)
        for a in (query, key_in, value)
    ]
    block = jnp.arange(frames, dtype=jnp.int32) // (frames // mask.shape[0])
    allowed = mask[block][:, block] > 0
    scores = jnp.einsum("iphd,jphd->phij", moved[0], moved[1], preferred_element_type=jnp.float32) / HDIM**0.5
    scores = jnp.where(allowed, scores, -1e30)
    expo = jnp.exp(scores - jnp.max(scores, axis=-1, keepdims=True))
    total = jnp.transpose(jnp.sum(expo, axis=-1), (2, 0, 1))[..., None]
    summed = jnp.einsum("phij,jphd->iphd", expo.astype(jnp.bfloat16), moved[2], preferred_element_type=jnp.float32)
    attended = (summed / total).astype(jnp.bfloat16).reshape(frames, width, feats)
    projected = jnp.dot(attended, w_out, preferred_element_type=jnp.float32).astype(jnp.bfloat16)
    back = lax.all_to_all(projected, AXES, split_axis=0, concat_axis=0, tiled=True)
    return back.reshape(query.shape)

def per_device(query, key_in, value, mask, w_out):
    _, _, patches, feats = query.shape
    n_tm, n_pix = lax.axis_size("tm"), lax.axis_size("pix")
    frames = n_tm * n_pix
    if n_pix % HI != 0 or patches != 4 * frames * SUB:
        return plain(query, key_in, value, mask, w_out)
    n_low = n_pix // HI
    plane = n_tm * n_low
    tall = 2 * SUB
    high = lax.axis_index("pix") // n_low
    teams = [[t * n_pix + z * n_low + x for t in range(n_tm) for x in range(n_low)] for z in range(HI)]
    order = [(p, t) for p in range(n_pix) for t in range(n_tm)]
    number = {device: i for i, device in enumerate(order)}
    tie = lax.optimization_barrier

    row = jnp.arange(HI * plane * SUB, dtype=jnp.int32)
    slot, source = row // (plane * SUB), row // SUB % plane
    frame = source // n_low * n_pix + (high ^ sum(jnp.where(slot == s, k, 0) for s, k in enumerate(NEAR))) * n_low + source % n_low
    blen = frames // mask.shape[0]
    always = mask[0, 0] >= 0

    def region(f, *args):
        shapes = jax.eval_shape(f, *args)
        return lax.cond(always, f, lambda *_: jax.tree.map(lambda s: jnp.zeros(s.shape, s.dtype), shapes), *args)

    def along(a, k):
        pairs = [(number[(p, t)], number[((p // n_low ^ k) * n_low + p % n_low, t)]) for p, t in order]
        return lax.ppermute(a, ("pix", "tm"), pairs)

    def across(a):
        return lax.all_to_all(a, AXES, split_axis=0, concat_axis=0, tiled=True, axis_index_groups=teams)

    flat = [a.reshape(patches // tall, tall, feats) for a in (query, key_in, value)]
    piece = (plane, 3, tall, feats)
    whole = (plane, HI, 3, tall, feats)

    def cut(slots):
        def body(z, ins, outs):
            return [
                [(a.at[pl.ds((z ^ k) * plane, plane)], out.at[:, t]) for t, a in enumerate(ins)]
                for k, out in zip(slots, outs)
            ]

        return lambda *flat: mover(body, flat, [piece] * len(slots), 3 * len(slots), high)

    far = cut(NEAR[1:])(*flat)
    far, flat = tie((far, flat))
    moved = [along(a, k) for a, k in zip(far, NEAR[1:])]

    def pack(z, ins, outs):
        return [
            [(a.at[1, :, y], outs[0].at[:, :, y, t]) for y in range(HI) for t, a in enumerate(ins)]
        ]

    def split(z, ins, outs):
        return [[(ins[0].at[:, z ^ k], out)] for k, out in zip(NEAR, outs)]

    def start_second(*flat):
        owned = [a.reshape(2, n_tm, HI, n_low, tall, feats) for a in flat]
        [packed] = mover(pack, owned, [(n_tm, n_low, *whole[1:])], 3 * HI, high)
        packed, flat = tie((packed.reshape(whole), flat))
        bias = bias_of(mask, frame, row % SUB, blen)
        return mover(split, [across(packed)], [piece] * HI, HI, high), cut((0,))(*flat), bias

    second, own, bias = region(start_second, *flat)
    late = NEAR.index(2)
    slots = [s for s in range(HI) if s != late]

    def each(z, ins, stages):
        return [[(a, stage)] for a, stage in zip(ins, stages)]

    def early_place(outs):
        return [outs[0].at[:, s] for s in slots]

    early = [[*own, *moved][s] for s in slots]
    packed = mover(each, early, [whole], HI - 1, high, [piece] * (HI - 1), early_place)
    second, packed, last = tie((second, packed, moved[late - 1]))
    second = [second[0], *[along(a, k) for a, k in zip(second[1:], NEAR[1:])]]
    [packed] = mover(each, [last, *packed], [whole], 1, high, [piece], lambda outs: [outs[0].at[:, late]], {2: 0})

    def finish_first(packed, bias, w_out):
        packed = across(packed).reshape(plane, HI, 3, 2, SUB, feats)
        return across(attend(high, [(packed, k) for k in range(HI)], bias, w_out))

    def finish_second(second, bias, w_out):
        second = [a.reshape(plane, 1, 3, 2, SUB, feats) for a in second]
        out = attend(high, [(a, 0) for a in second], bias, w_out, n_tm)
        return lax.all_to_all(out.reshape(frames, tall, feats), AXES, split_axis=0, concat_axis=0, tiled=True)

    def give_back(done):
        pieces = [done[:, k].reshape(plane * tall, feats) for k in range(HI)]
        return [pieces[0], *[along(a, k) for a, k in zip(pieces[1:], NEAR[1:])]]

    done_first = region(finish_first, packed, bias, w_out)
    second, done_first = tie((second, done_first))
    back_first = give_back(done_first)
    done_second = region(finish_second, second, bias, w_out)
    back_first, done_second = tie((back_first, done_second))
    upper = jnp.zeros((HI, plane * tall, feats), jnp.bfloat16)
    for k, back in zip(NEAR, back_first):
        upper = lax.dynamic_update_index_in_dim(upper, back, high ^ k, 0)
    result = jnp.concatenate([upper, done_second.reshape(HI, plane * tall, feats)], axis=0)
    return result.reshape(query.shape)


def solution(mesh):
    placed = P("tm", "pix", None, None)
    return jax.shard_map(
        per_device, mesh=mesh, in_specs=(placed, placed, placed, P(), P()), out_specs=placed, check_vma=False
    )
```

```python
import functools
import math

import jax
import jax.numpy as jnp
from jax import lax
from jax.experimental import pallas as pl
from jax.experimental.pallas import tpu as pltpu
from jax.sharding import PartitionSpec as P

HDIM = 72
LANES = 128
SUB = 8
HI = 4
NEAR = (0, 3, 1, 2)
AXES = ("tm", "pix")


def mover(body, arrays, out_shapes, number, scalar, stage_shapes=None, place=None, aliases=None):
    count, outs = len(arrays), len(out_shapes)
    stage_shapes = stage_shapes or out_shapes
    place = place or (lambda out_refs: out_refs)

    def kernel(z_ref, *refs):
        sems, out_sems = refs[-2:]
        stages, targets = refs[count + outs : -2], place(refs[count : count + outs])
        arriving, slot = [], 0
        for pairs in body(z_ref[0], refs[:count], stages):
            arriving.append([pltpu.make_async_copy(a, b, sems.at[slot + i]) for i, (a, b) in enumerate(pairs)])
            slot += len(pairs)
        leaving = [pltpu.make_async_copy(a, b, out_sems.at[i]) for i, (a, b) in enumerate(zip(stages, targets))]
        for copy in sum(arriving, []):
            copy.start()
        for copies, out in zip(arriving, leaving):
            for copy in copies:
                copy.wait()
            out.start()
        for out in leaving:
            out.wait()

    return pl.pallas_call(
        kernel,
        grid_spec=pltpu.PrefetchScalarGridSpec(
            num_scalar_prefetch=1,
            in_specs=[pl.BlockSpec(memory_space=pl.ANY)] * count,
            out_specs=[pl.BlockSpec(memory_space=pl.ANY)] * outs,
            scratch_shapes=[pltpu.VMEM(s, jnp.bfloat16) for s in stage_shapes]
            + [pltpu.SemaphoreType.DMA((number,)), pltpu.SemaphoreType.DMA((len(stage_shapes),))],
        ),
        out_shape=[jax.ShapeDtypeStruct(s, jnp.bfloat16) for s in out_shapes],
        input_output_aliases=aliases or {},
        cost_estimate=pl.CostEstimate(flops=0, bytes_accessed=0, transcendentals=0),
    )(scalar.reshape(1), *arrays)


def attend_kernel(by_frame, z_ref, *refs):
    slots, (bias_ref, w_hbm, out_ref, acc_ref, w_ref, w_sem) = refs[:HI], refs[HI:]
    rows, feats = acc_ref.shape
    part = rows // HI
    scale = math.log2(math.e) / HDIM**0.5
    fetch = pltpu.make_async_copy(w_hbm, w_ref, w_sem)

    @pl.when(pl.program_id(0) == 0)
    def _():
        fetch.start()

    def load(which, start, stop):
        pieces = [s[:, 0, which, 0, :, start:stop].reshape(part, stop - start) for s in slots]
        return jnp.concatenate(pieces, axis=0)

    heads = feats // HDIM

    def window(head):
        low, high = head * HDIM, (head + 1) * HDIM
        start, stop = low // LANES * LANES, -(-high // LANES) * LANES
        lane = lax.broadcasted_iota(jnp.int32, (1, stop - start), 1) + start
        return start, stop, (lane >= low) & (lane < high)

    def score(head):
        start, stop, mine = window(head)
        q, k = load(0, start, stop), load(1, start, stop)
        q = jnp.where(mine, q, jnp.zeros_like(q))
        return lax.dot_general(q, k, (((1,), (1,)), ((), ())), preferred_element_type=jnp.float32)

    def weigh(scores):
        scores = scores * scale + bias_ref[...]
        expo = jnp.exp2(scores - jnp.max(scores, axis=1, keepdims=True))
        return expo.astype(jnp.bfloat16), 1.0 / jnp.sum(expo, axis=1, keepdims=True)

    def blend(head, expo, share):
        start, stop, mine = window(head)
        summed = jnp.dot(expo, load(2, start, stop), preferred_element_type=jnp.float32)
        acc_ref[:, start:stop] = jnp.where(mine, (summed * share).astype(jnp.bfloat16), acc_ref[:, start:stop])

    scores = score(0)
    for head in range(heads):
        later = score(head + 1) if head + 1 < heads else None
        expo, share = weigh(scores)
        blend(head, expo, share)
        scores = later
    @pl.when(pl.program_id(0) == 0)
    def _():
        fetch.wait()

    projected = jnp.dot(acc_ref[...], w_ref[...], preferred_element_type=jnp.float32).astype(jnp.bfloat16)
    for slot, k in enumerate(NEAR):
        own = projected[slot * part : (slot + 1) * part]
        if by_frame:
            out_ref[:, z_ref[0] ^ k, :, 0] = own.reshape(out_ref.shape[0], out_ref.shape[2], SUB, feats)
        else:
            out_ref[:, slot, 0] = own.reshape(out_ref.shape[0], SUB, feats)


def attend(place, slots, bias, w_out, outer=None):
    sources, _, _, groups, sub, feats = slots[0][0].shape
    rows = HI * sources * sub

    shape = (sources, HI) if outer is None else (outer, HI, sources // outer)
    zeros = (0,) * len(shape)

    def spec(entry):
        return pl.BlockSpec((sources, 1, 3, 1, sub, feats), lambda g, z: (0, entry, 0, g, 0, 0))

    return pl.pallas_call(
        functools.partial(attend_kernel, outer is not None),
        grid_spec=pltpu.PrefetchScalarGridSpec(
            num_scalar_prefetch=1,
            grid=(groups,),
            in_specs=[spec(entry) for _, entry in slots]
            + [pl.BlockSpec((rows, rows), lambda g, z: (0, 0)), pl.BlockSpec(memory_space=pl.ANY)],
            out_specs=pl.BlockSpec((*shape, 1, sub, feats), lambda g, z: (*zeros, g, 0, 0)),
            scratch_shapes=[
                pltpu.VMEM((rows, feats), jnp.bfloat16),
                pltpu.VMEM((feats, feats), jnp.bfloat16),
                pltpu.SemaphoreType.DMA,
            ],
        ),
        out_shape=jax.ShapeDtypeStruct((*shape, groups, sub, feats), jnp.bfloat16),
        compiler_params=pltpu.CompilerParams(vmem_limit_bytes=48 * 2**20),
        cost_estimate=pl.CostEstimate(flops=0, bytes_accessed=0, transcendentals=0),
    )(place.reshape(1), *[a for a, _ in slots], bias, w_out)


def bias_of(mask, frame_of_row, patch_of_row, blen):
    block = frame_of_row // blen
    hot = (block[:, None] == jnp.arange(mask.shape[0], dtype=jnp.int32)).astype(jnp.float32)
    allowed = jnp.dot(jnp.dot(hot, mask.astype(jnp.float32)), hot.T) > 0.5
    return jnp.where(allowed & (patch_of_row[:, None] == patch_of_row[None, :]), 0.0, -1e30).astype(jnp.float32)


def plain(query, key_in, value, mask, w_out):
    _, _, patches, feats = query.shape
    frames = lax.axis_size(AXES)
    width, heads = patches // frames, feats // HDIM
    moved = [
        lax.all_to_all(a.reshape(frames, width, feats), AXES, split_axis=0, concat_axis=0, tiled=True)
        .reshape(frames, width, heads, HDIM)
        for a in (query, key_in, value)
    ]
    block = jnp.arange(frames, dtype=jnp.int32) // (frames // mask.shape[0])
    allowed = mask[block][:, block] > 0
    scores = jnp.einsum("iphd,jphd->phij", moved[0], moved[1], preferred_element_type=jnp.float32) / HDIM**0.5
    scores = jnp.where(allowed, scores, -1e30)
    expo = jnp.exp(scores - jnp.max(scores, axis=-1, keepdims=True))
    total = jnp.transpose(jnp.sum(expo, axis=-1), (2, 0, 1))[..., None]
    summed = jnp.einsum("phij,jphd->iphd", expo.astype(jnp.bfloat16), moved[2], preferred_element_type=jnp.float32)
    attended = (summed / total).astype(jnp.bfloat16).reshape(frames, width, feats)
    projected = jnp.dot(attended, w_out, preferred_element_type=jnp.float32).astype(jnp.bfloat16)
    back = lax.all_to_all(projected, AXES, split_axis=0, concat_axis=0, tiled=True)
    return back.reshape(query.shape)

def per_device(query, key_in, value, mask, w_out):
    _, _, patches, feats = query.shape
    n_tm, n_pix = lax.axis_size("tm"), lax.axis_size("pix")
    frames = n_tm * n_pix
    if n_pix % HI != 0 or patches != 4 * frames * SUB:
        return plain(query, key_in, value, mask, w_out)
    n_low = n_pix // HI
    plane = n_tm * n_low
    tall = 2 * SUB
    high = lax.axis_index("pix") // n_low
    teams = [[t * n_pix + z * n_low + x for t in range(n_tm) for x in range(n_low)] for z in range(HI)]
    order = [(p, t) for p in range(n_pix) for t in range(n_tm)]
    number = {device: i for i, device in enumerate(order)}
    tie = lax.optimization_barrier

    row = jnp.arange(HI * plane * SUB, dtype=jnp.int32)
    slot, source = row // (plane * SUB), row // SUB % plane
    frame = source // n_low * n_pix + (high ^ sum(jnp.where(slot == s, k, 0) for s, k in enumerate(NEAR))) * n_low + source % n_low
    blen = frames // mask.shape[0]
    always = mask[0, 0] >= 0

    def region(f, *args):
        shapes = jax.eval_shape(f, *args)
        return lax.cond(always, f, lambda *_: jax.tree.map(lambda s: jnp.zeros(s.shape, s.dtype), shapes), *args)

    def along(a, k):
        pairs = [(number[(p, t)], number[((p // n_low ^ k) * n_low + p % n_low, t)]) for p, t in order]
        return lax.ppermute(a, ("pix", "tm"), pairs)

    def across(a):
        return lax.all_to_all(a, AXES, split_axis=0, concat_axis=0, tiled=True, axis_index_groups=teams)

    flat = [a.reshape(patches // tall, tall, feats) for a in (query, key_in, value)]
    piece = (plane, 3, tall, feats)
    whole = (plane, HI, 3, tall, feats)

    def cut(slots):
        def body(z, ins, outs):
            return [
                [(a.at[pl.ds((z ^ k) * plane, plane)], out.at[:, t]) for t, a in enumerate(ins)]
                for k, out in zip(slots, outs)
            ]

        return lambda *flat: mover(body, flat, [piece] * len(slots), 3 * len(slots), high)

    far = cut(NEAR[1:])(*flat)
    far, flat = tie((far, flat))
    moved = [along(a, k) for a, k in zip(far, NEAR[1:])]

    def pack(z, ins, outs):
        return [
            [(a.at[1, :, y], outs[0].at[:, :, y, t]) for y in range(HI) for t, a in enumerate(ins)]
        ]

    def split(z, ins, outs):
        return [[(ins[0].at[:, z ^ k], out)] for k, out in zip(NEAR, outs)]

    def start_second(*flat):
        owned = [a.reshape(2, n_tm, HI, n_low, tall, feats) for a in flat]
        [packed] = mover(pack, owned, [(n_tm, n_low, *whole[1:])], 3 * HI, high)
        packed, flat = tie((packed.reshape(whole), flat))
        bias = bias_of(mask, frame, row % SUB, blen)
        return mover(split, [across(packed)], [piece] * HI, HI, high), cut((0,))(*flat), bias

    second, own, bias = region(start_second, *flat)
    late = NEAR.index(2)
    slots = [s for s in range(HI) if s != late]

    def each(z, ins, stages):
        return [[(a, stage)] for a, stage in zip(ins, stages)]

    def early_place(outs):
        return [outs[0].at[:, s] for s in slots]

    early = [[*own, *moved][s] for s in slots]
    packed = mover(each, early, [whole], HI - 1, high, [piece] * (HI - 1), early_place)
    second, packed, last = tie((second, packed, moved[late - 1]))
    second = [second[0], *[along(a, k) for a, k in zip(second[1:], NEAR[1:])]]
    [packed] = mover(each, [last, *packed], [whole], 1, high, [piece], lambda outs: [outs[0].at[:, late]], {2: 0})

    def finish_first(packed, bias, w_out):
        packed = across(packed).reshape(plane, HI, 3, 2, SUB, feats)
        return across(attend(high, [(packed, k) for k in range(HI)], bias, w_out))

    def finish_second(second, bias, w_out):
        second = [a.reshape(plane, 1, 3, 2, SUB, feats) for a in second]
        out = attend(high, [(a, 0) for a in second], bias, w_out, n_tm)
        return lax.all_to_all(out.reshape(frames, tall, feats), AXES, split_axis=0, concat_axis=0, tiled=True)

    def give_back(done):
        pieces = [done[:, k].reshape(plane * tall, feats) for k in range(HI)]
        return [pieces[0], *[along(a, k) for a, k in zip(pieces[1:], NEAR[1:])]]

    done_first = region(finish_first, packed, bias, w_out)
    second, done_first = tie((second, done_first))
    back_first = give_back(done_first)
    done_second = region(finish_second, second, bias, w_out)
    back_first, done_second = tie((back_first, done_second))
    upper = jnp.zeros((HI, plane * tall, feats), jnp.bfloat16)
    for k, back in zip(NEAR, back_first):
        upper = lax.dynamic_update_index_in_dim(upper, back, high ^ k, 0)
    result = jnp.concatenate([upper, done_second.reshape(HI, plane * tall, feats)], axis=0)
    return result.reshape(query.shape)


def solution(mesh):
    placed = P("tm", "pix", None, None)
    return jax.shard_map(
        per_device, mesh=mesh, in_specs=(placed, placed, placed, P(), P()), out_specs=placed, check_vma=False
    )
```
